32 devices in a mesh: mom: 8 (over z, y), idx: 4 (over x, core).
Axes of the slice: x: 2, y: 2, z: 4, core: 2. Of those that a mesh axis runs over, the one named last changes fastest.
Arguments:
- vertex: bfloat16 [3, 256, 512, 512], P(None, 'mom', None, 'idx'), may hold values from -0.25 to 0.25
- formfactors: bfloat16 [2048, 512], replicated, may hold values from -6 to 6
- propagator: float32 [256], replicated, may hold values from -4 to 4
- loop_mom: int32 [2048], replicated, may hold values from 0 to 255
- bond_disp: int32 [8, 2], replicated, may hold values from 0 to 15
- proj_channel: int32 [3, 8, 4], replicated, may hold values from 0 to 2
- proj_bond: int32 [3, 8, 4], replicated, may hold values from 0 to 7
- proj_phase: int32 [3, 8, 4], replicated, may hold values from 0 to 3
Outputs:
- flow: float32 [3, 256, 512, 512], P(None, 'mom', None, 'idx')
The draws below stay inside these ranges and needn't reach their ends.
All inputs are finite; a program needn't handle non-finite values.
Results may differ from the reference program's by a relative error of at most 0.005.
Values may be sent and summed in bfloat16 or wider, within the bound.
A program may use at most 192 MiB of HBM per device.

```python
import math
import jax
import jax.numpy as jnp
from jax import lax

MSIDE = 16
NQ = 256
NI = 512
NL = 2048
NB = 8
SOURCES = 4


def place_ends(entries, stream_key, low, top_value):
    longest = entries.shape.index(max(entries.shape))
    spots = []
    for shift in (0, 1):
        where = [jax.random.randint(jax.random.fold_in(stream_key, axis), (), 0, length) for axis, length in enumerate(entries.shape)]
        where[longest] = (where[longest] + shift) % entries.shape[longest]
        spots.append(tuple(where))
    return entries.at[spots[0]].set(low).at[spots[1]].set(top_value)


def steps_of(rng, extent, split, least, largest):
    def one(position, shards_of):
        steps = jax.random.uniform(jax.random.fold_in(jax.random.fold_in(rng, 6), position), (shards_of,), jnp.float32, least / len(split), largest / len(split))
        return jnp.repeat(jnp.exp(steps), extent[position] // shards_of).reshape((-1,) + (1,) * (len(extent) - position - 1))

    factor_of = one(*split[0])
    for cut in split[1:]:
        factor_of = factor_of * one(*cut)
    return factor_of


def scatter_about(rng, shape, width, most, pieces=(), kind=jnp.bfloat16):
    entries = width * jax.random.normal(rng, shape, jnp.float32)
    if pieces:
        entries = entries * steps_of(rng, shape, pieces, -0.22, 0.18)
    return jnp.clip(entries, -most, most).astype(kind)


def setup_inputs(seed: int = 0) -> dict:
    key_list = jax.random.split(jax.random.key(seed), 9)
    vertex = scatter_about(key_list[0], (3, NQ, NI, NI), NI ** -0.5, 0.25, ((1, 8), (3, 4)))
    formfactors = scatter_about(key_list[1], (NL, NI), 1.0, 6.0)
    propagator = scatter_about(key_list[2], (NQ,), 1.0, 4.0, (), jnp.float32)
    loop_mom = place_ends(jax.random.randint(key_list[3], (NL,), 0, NQ), jax.random.fold_in(key_list[3], 1), 0, NQ - 1).astype(jnp.int32)
    bond_disp = place_ends(jax.random.randint(key_list[4], (NB, 2), 0, MSIDE), jax.random.fold_in(key_list[4], 1), 0, MSIDE - 1).astype(jnp.int32)
    proj_channel = place_ends(jax.random.randint(key_list[5], (3, NB, SOURCES), 0, 3), jax.random.fold_in(key_list[5], 1), 0, 2).astype(jnp.int32)
    proj_bond = place_ends(jax.random.randint(key_list[6], (3, NB, SOURCES), 0, NB), jax.random.fold_in(key_list[6], 1), 0, NB - 1).astype(jnp.int32)
    proj_phase = place_ends(jax.random.randint(key_list[7], (3, NB, SOURCES), 0, 4), jax.random.fold_in(key_list[7], 1), 0, 3).astype(jnp.int32)
    return dict(vertex=vertex, formfactors=formfactors, propagator=propagator, loop_mom=loop_mom, bond_disp=bond_disp, proj_channel=proj_channel, proj_bond=proj_bond, proj_phase=proj_phase)


def momentum_sum(former, latter, signed):
    coord_x = (former // MSIDE + signed * (latter // MSIDE)) % MSIDE
    coord_y = (former % MSIDE + signed * (latter % MSIDE)) % MSIDE
    return (coord_x * MSIDE + coord_y).astype(jnp.int32)

def loop_weights(propagator, loop_mom, momenta):
    pair = momentum_sum(momenta[:, None], loop_mom[None, :], -1)
    plus = momentum_sum(loop_mom[None, :], momenta[:, None], 1)
    minus = momentum_sum(loop_mom[None, :], momenta[:, None], -1)
    own = propagator[loop_mom][None, :]
    return jnp.stack([own * propagator[pair], own * propagator[plus], own * propagator[minus]])

def phase_table(bond_disp, momenta):
    coord_x = momenta // MSIDE
    coord_y = momenta % MSIDE
    turns = (bond_disp[:, 0:1] * coord_x[None, :] + bond_disp[:, 1:2] * coord_y[None, :]) % MSIDE
    angles = turns.astype(jnp.float32) * (2.0 * math.pi / MSIDE)
    return jnp.stack([jnp.cos(angles), -jnp.sin(angles)]).astype(jnp.bfloat16)

def mixing_tables(proj_channel, proj_bond, proj_phase):
    chan_hot = (proj_channel[..., None] == jnp.arange(3, dtype=jnp.int32)).astype(jnp.float32)
    bond_hot = (proj_bond[..., None] == jnp.arange(proj_bond.shape[1], dtype=jnp.int32)).astype(jnp.float32)
    direct = (proj_phase == 0).astype(jnp.float32) - (proj_phase == 2).astype(jnp.float32)
    crossed = (proj_phase == 3).astype(jnp.float32) - (proj_phase == 1).astype(jnp.float32)
    same = jnp.einsum('xysu,xysv,xys->xyuv', chan_hot, bond_hot, direct, precision=lax.Precision.HIGHEST)
    swapped = jnp.einsum('xysu,xysv,xys->xyuv', chan_hot, bond_hot, crossed, precision=lax.Precision.HIGHEST)
    return (same, swapped)

def reference(vertex, formfactors, propagator, loop_mom, bond_disp, proj_channel, proj_bond, proj_phase):
    momenta = jnp.arange(NQ, dtype=jnp.int32)
    weights = loop_weights(propagator, loop_mom, momenta)
    scale_nl = 1.0 / math.sqrt(NL)
    form_wide = formfactors.astype(jnp.float32)

    def per_momentum(index):
        vertex_q = lax.dynamic_index_in_dim(vertex, index, 1, keepdims=False).astype(jnp.float32)
        weight_q = lax.dynamic_index_in_dim(weights, index, 1, keepdims=False)
        loop_terms = jnp.einsum('li,cij->clj', form_wide, vertex_q, precision=lax.Precision.HIGHEST)
        weighted = (loop_terms * weight_q[:, :, None] * scale_nl).astype(jnp.bfloat16)
        weighted = lax.optimization_barrier(weighted).astype(jnp.float32)
        kernel = jnp.einsum('li,clj->cij', form_wide, weighted, precision=lax.Precision.HIGHEST).astype(jnp.bfloat16)
        kernel = lax.optimization_barrier(kernel).astype(jnp.float32)
        return jnp.einsum('cia,caj->cij', vertex_q, kernel, precision=lax.Precision.HIGHEST)
    increment = lax.map(per_momentum, momenta)
    increment_b = lax.optimization_barrier(increment.astype(jnp.bfloat16)).astype(jnp.float32)
    phases = phase_table(bond_disp, momenta).astype(jnp.float32)
    bond_terms = jnp.einsum('pbq,qcij->icpbj', phases, increment_b, precision=lax.Precision.HIGHEST) * (1.0 / MSIDE)
    same, swapped = mixing_tables(proj_channel, proj_bond, proj_phase)
    real_part = bond_terms[:, :, 0]
    imag_part = bond_terms[:, :, 1]

    def mixing(table, values):
        return jnp.einsum('xyuv,iuvj->ixyj', table, values, precision=lax.Precision.HIGHEST)
    proj_real = mixing(same, real_part) + mixing(swapped, imag_part)
    proj_imag = mixing(same, imag_part) - mixing(swapped, real_part)
    projected = jnp.stack([proj_real, proj_imag], axis=2).astype(jnp.bfloat16)
    projected = lax.optimization_barrier(projected).astype(jnp.float32)
    back_scale = 1.0 / math.sqrt(NB * SOURCES)
    returned = jnp.einsum('pbq,icpbj->qcij', phases, projected, precision=lax.Precision.HIGHEST) * back_scale
    flow = increment + returned
    return jnp.moveaxis(flow, 0, 1)
```

```python
import functools
import math

import jax
import jax.numpy as jnp
from jax import lax
from jax.experimental import pallas as pl
from jax.experimental.pallas import tpu as pltpu
from jax.sharding import PartitionSpec as P

MSIDE = 16
VMEM = 56 * 1024 * 1024
GROUP = 16
DEPTH = 2
CHUNKS = (4, 4, 4, 2, 2)


def momentum_sum(former, latter, signed):
    coord_x = (former // MSIDE + signed * (latter // MSIDE)) % MSIDE
    coord_y = (former % MSIDE + signed * (latter % MSIDE)) % MSIDE
    return coord_x * MSIDE + coord_y


def lookup(values, indices):
    hits = indices[..., None] == jnp.arange(values.shape[0], dtype=jnp.int32)
    return jnp.sum(jnp.where(hits, values, 0.0), axis=-1)


def loop_weights(propagator, loop_mom, momenta):
    every = jnp.arange(propagator.shape[0], dtype=jnp.int32)
    pair = momentum_sum(momenta[:, None], every[None, :], -1)
    plus = momentum_sum(every[None, :], momenta[:, None], 1)
    minus = momentum_sum(every[None, :], momenta[:, None], -1)
    table = propagator * lookup(propagator, jnp.stack([pair, plus, minus]))
    hits = (every[:, None] == loop_mom[None, :]).astype(jnp.float32)
    return jnp.einsum("cqk,kl->cql", table, hits, precision=lax.Precision.HIGHEST)


def phase_table(bond_disp, momenta):
    coord_x = momenta // MSIDE
    coord_y = momenta % MSIDE
    turns = (bond_disp[:, 0:1] * coord_x[None, :] + bond_disp[:, 1:2] * coord_y[None, :]) % MSIDE
    angles = turns.astype(jnp.float32) * (2.0 * math.pi / MSIDE)
    return jnp.stack([jnp.cos(angles), -jnp.sin(angles)]).astype(jnp.bfloat16)


def mixing_tables(proj_channel, proj_bond, proj_phase):
    chan_hot = (proj_channel[..., None] == jnp.arange(3, dtype=jnp.int32)).astype(jnp.float32)
    bond_hot = (proj_bond[..., None] == jnp.arange(proj_bond.shape[1], dtype=jnp.int32)).astype(
        jnp.float32
    )
    direct = (proj_phase == 0).astype(jnp.float32) - (proj_phase == 2).astype(jnp.float32)
    crossed = (proj_phase == 3).astype(jnp.float32) - (proj_phase == 1).astype(jnp.float32)
    same = jnp.einsum(
        "xysu,xysv,xys->xyuv", chan_hot, bond_hot, direct, precision=lax.Precision.HIGHEST
    )
    swapped = jnp.einsum(
        "xysu,xysv,xys->xyuv", chan_hot, bond_hot, crossed, precision=lax.Precision.HIGHEST
    )
    return (same, swapped)


def kernel_body(v_ref, w_ref, ft_ref, ff_ref, out_ref, acc_ref):
    count = v_ref.shape[1]
    width = v_ref.shape[3]
    turned = jnp.concatenate([v_ref[0, q].T for q in range(count)], axis=0)
    step = ff_ref.shape[0] // 4
    acc_ref[...] = jnp.zeros_like(acc_ref)

    def part(index, carry):
        at = pl.ds(pl.multiple_of(index * step, step), step)
        terms = jnp.dot(turned, ft_ref[:, at], preferred_element_type=jnp.float32)
        weighted = terms.reshape(count, width, step) * w_ref[0, 0, :, at][:, None, :]
        weighted = weighted.reshape(count * width, step).astype(jnp.bfloat16)
        acc_ref[...] += jnp.dot(weighted, ff_ref[at, :], preferred_element_type=jnp.float32)
        return carry

    lax.fori_loop(0, 4, part, 0)
    out_ref[0] = acc_ref[...].astype(jnp.bfloat16).reshape(count, width, -1)


def bubble(channel, vertex, weights, forms_t, forms):
    _, count_q, rows, width = vertex.shape
    loops = forms.shape[0]
    block = math.gcd(count_q, 4)
    weights = weights.reshape(weights.shape[0], count_q // block, block, loops)
    return pl.pallas_call(
        kernel_body,
        grid=(count_q // block,),
        in_specs=[
            pl.BlockSpec((1, block, rows, width), lambda s: (channel, s, 0, 0)),
            pl.BlockSpec((1, 1, block, loops), lambda s: (channel, s, 0, 0)),
            pl.BlockSpec(forms_t.shape, lambda s: (0, 0)),
            pl.BlockSpec(forms.shape, lambda s: (0, 0)),
        ],
        out_specs=pl.BlockSpec((1, block, width, rows), lambda s: (0, s, 0, 0)),
        out_shape=jax.ShapeDtypeStruct((1, count_q, width, rows), jnp.bfloat16),
        scratch_shapes=[pltpu.VMEM((block * width, rows), jnp.float32)],
        compiler_params=pltpu.CompilerParams(vmem_limit_bytes=VMEM),
        cost_estimate=pl.CostEstimate(
            flops=4 * count_q * rows * width * loops,
            bytes_accessed=4 * count_q * rows * width,
            transcendentals=0,
        ),
    )(vertex, weights, forms_t, forms)


def step_body(slots, *refs):
    panels = refs[:slots]
    kernels = refs[slots : slots + 3]
    there_ref, inc_ref, bond_ref = refs[slots + 3 :]
    channel = pl.program_id(0)
    count_q, rows, width = inc_ref.shape[1:]
    for choice in range(3):

        @pl.when(channel == choice)
        def _():
            def one(q, carry):
                left = jnp.concatenate([panel[0, q] for panel in panels], axis=1)
                product = lax.dot_general(
                    left,
                    kernels[choice][0, q],
                    (((1,), (1,)), ((), ())),
                    preferred_element_type=jnp.float32,
                )
                inc_ref[0, q] = product.astype(jnp.bfloat16)
                return carry

            lax.fori_loop(0, count_q, one, 0, unroll=4)

    for start in range(0, rows, GROUP):
        piece = inc_ref[0, :, start : start + GROUP, :].reshape(count_q * GROUP, width)
        terms = jnp.dot(there_ref[...], piece, preferred_element_type=jnp.float32)
        bond_ref[0, :, start : start + GROUP, :] = terms.astype(jnp.bfloat16).reshape(
            -1, GROUP, width
        )


def increments(first, size, vertex, others, kernels, there):
    chans, count_q, rows_all, width = vertex.shape
    slots = 1 + len(others)
    terms = there.shape[0] // GROUP
    block = math.gcd(math.gcd(first, size), 128)
    lead = first // block
    kernel_spec = pl.BlockSpec(
        (1, count_q, width, rows_all), lambda c, s: (0, 0, 0, 0), pipeline_mode=pl.Buffered(1)
    )
    return pl.pallas_call(
        functools.partial(step_body, slots),
        grid=(chans, size // block),
        in_specs=[pl.BlockSpec((1, count_q, block, width), lambda c, s: (c, 0, s + lead, 0))]
        + [pl.BlockSpec((1, count_q, block, width), lambda c, s: (c, 0, s, 0))] * len(others)
        + [kernel_spec] * 3
        + [pl.BlockSpec(there.shape, lambda c, s: (0, 0))],
        out_specs=[
            pl.BlockSpec((1, count_q, block, width), lambda c, s: (c, 0, s, 0)),
            pl.BlockSpec((1, terms, block, width), lambda c, s: (c, 0, s, 0)),
        ],
        out_shape=[
            jax.ShapeDtypeStruct((chans, count_q, size, width), jnp.bfloat16),
            jax.ShapeDtypeStruct((chans, terms, size, width), jnp.bfloat16),
        ],
        compiler_params=pltpu.CompilerParams(vmem_limit_bytes=VMEM),
        cost_estimate=pl.CostEstimate(
            flops=8 * chans * count_q * rows_all * width * size,
            bytes_accessed=2 * chans * count_q * width * (rows_all + size * (slots + 1)),
            transcendentals=0,
        ),
    )(vertex, *others, *kernels, there)


def flow_body(scale, *refs):
    inc_ref, proj_ref, back_ref = refs[:3]
    out_ref = refs[-1]
    count_q, rows, width = inc_ref.shape[1:]
    terms = proj_ref.shape[1]
    for start in range(0, rows, GROUP):
        at = slice(start, start + GROUP)
        piece = proj_ref[0, :, at, :].reshape(terms * GROUP, width)
        back = jnp.dot(back_ref[...], piece, preferred_element_type=jnp.float32) * scale
        out_ref[0, :, at, :] = inc_ref[0, :, at, :].astype(jnp.float32) + back.reshape(
            count_q, GROUP, width
        )


def finish(first, flow, shape, inc, projected, back, scale):
    chans, count_q, size, width = inc.shape
    terms = projected.shape[1]
    block = math.gcd(math.gcd(first, size), 64)
    lead = first // block
    extra = [] if flow is None else [flow]
    return pl.pallas_call(
        functools.partial(flow_body, scale),
        grid=(chans, size // block),
        in_specs=[
            pl.BlockSpec((1, count_q, block, width), lambda c, s: (c, 0, s, 0)),
            pl.BlockSpec((1, terms, block, width), lambda c, s: (c, 0, s, 0)),
            pl.BlockSpec(back.shape, lambda c, s: (0, 0)),
        ]
        + [pl.BlockSpec(memory_space=pl.ANY)] * len(extra),
        out_specs=pl.BlockSpec((1, count_q, block, width), lambda c, s: (c, 0, s + lead, 0)),
        out_shape=jax.ShapeDtypeStruct(shape, jnp.float32),
        input_output_aliases={3: 0} if extra else {},
        compiler_params=pltpu.CompilerParams(vmem_limit_bytes=VMEM),
        cost_estimate=pl.CostEstimate(
            flops=2 * chans * count_q * size * width * terms * GROUP,
            bytes_accessed=6 * chans * count_q * size * width,
            transcendentals=0,
        ),
    )(inc, projected, back, *extra)


def swap(values, axis, count, bit):
    return lax.ppermute(values, axis, [(d, d ^ bit) for d in range(count)])


def bits_of(count):
    return [1 << k for k in range(count.bit_length() - 1)]


def scatter_sum(values, count):
    me = lax.axis_index("mom")
    for bit in bits_of(count):
        half = values.shape[2] // 2
        side = (me // bit) % 2
        mine = lax.dynamic_slice_in_dim(values, side * half, half, 2)
        theirs = lax.dynamic_slice_in_dim(values, (1 - side) * half, half, 2)
        got = swap(theirs, "mom", count, bit)
        total = mine.astype(jnp.float32) + got.astype(jnp.float32)
        values = total if bit * 2 == count else total.astype(jnp.bfloat16)
    return values.astype(jnp.float32)


def gather_rows(values, count):
    me = lax.axis_index("mom")
    for bit in reversed(bits_of(count)):
        side = (me // bit) % 2
        got = swap(values, "mom", count, bit)
        values = jnp.where(
            side == 0,
            jnp.concatenate([values, got], axis=2),
            jnp.concatenate([got, values], axis=2),
        )
    return values


def local(
    count_mom,
    count_idx,
    vertex,
    formfactors,
    propagator,
    loop_mom,
    bond_disp,
    proj_channel,
    proj_bond,
    proj_phase,
):
    chans, count_q, rows, width = vertex.shape
    parts = sum(CHUNKS)
    sizes = [rows * c // parts for c in CHUNKS]
    firsts = [sum(sizes[:k]) for k in range(len(sizes))]

    far = count_idx // 2
    held = []
    for k, (first, size) in enumerate(zip(firsts, sizes)):
        own = vertex[:, :, first : first + size, :]
        if k >= DEPTH:
            own, held[k - DEPTH][far] = lax.optimization_barrier((own, held[k - DEPTH][far]))
        slots = {0: own}
        for bit in reversed(bits_of(count_idx)):
            for slot in list(slots):
                slots[slot ^ bit] = swap(slots[slot], "idx", count_idx, bit)
        held.append(slots)

    q_ids = lax.axis_index("mom") * count_q + jnp.arange(count_q, dtype=jnp.int32)
    weights = loop_weights(propagator, loop_mom, q_ids) * (1.0 / math.sqrt(formfactors.shape[0]))
    me = lax.axis_index("idx")
    forms = jnp.concatenate(
        [
            lax.dynamic_slice_in_dim(formfactors, (me ^ slot) * width, width, 1)
            for slot in range(count_idx)
        ],
        axis=1,
    )
    forms_t = formfactors.T
    kernels = [bubble(c, vertex, weights, forms_t, forms) for c in range(chans)]

    bonds = bond_disp.shape[0]
    phases = phase_table(bond_disp, q_ids).reshape(2 * bonds, count_q)
    eye = jnp.eye(GROUP, dtype=jnp.bfloat16)
    there = jnp.einsum("tq,rs->trqs", phases * (1.0 / MSIDE), eye)
    there = there.astype(jnp.bfloat16).reshape(2 * bonds * GROUP, count_q * GROUP)
    back = jnp.einsum("tq,rs->qrts", phases, eye)
    back = back.astype(jnp.bfloat16).reshape(count_q * GROUP, 2 * bonds * GROUP)
    scale = 1.0 / math.sqrt(bonds * proj_channel.shape[2])
    same, swapped = mixing_tables(proj_channel, proj_bond, proj_phase)
    table = jnp.stack(
        [jnp.stack([same, swapped], axis=3), jnp.stack([-swapped, same], axis=3)], axis=1
    ).reshape(chans * 2 * bonds, chans * 2 * bonds)

    flow = None
    for first, size, slots in zip(firsts, sizes, held):
        others = [slots[slot] for slot in range(1, count_idx)]
        inc, bond = increments(first, size, vertex, others, kernels, there)
        summed = scatter_sum(bond, count_mom)
        mixed = jnp.einsum(
            "xk,krj->xrj",
            table,
            summed.reshape(table.shape[0], -1, width),
            precision=lax.Precision.HIGHEST,
        )
        projected = gather_rows(mixed.astype(jnp.bfloat16).reshape(summed.shape), count_mom)
        flow = finish(first, flow, vertex.shape, inc, projected, back, scale)
    return flow


def solution(mesh):
    in_specs = (P(None, "mom", None, "idx"), P(), P(), P(), P(), P(), P(), P())
    out_specs = P(None, "mom", None, "idx")
    body = functools.partial(local, mesh.shape["mom"], mesh.shape["idx"])
    return jax.shard_map(body, mesh=mesh, in_specs=in_specs, out_specs=out_specs, check_vma=False)
```
